32 devices in a mesh: src: 4 (over x, core), rcv: 8 (over z, y).
Axes of the slice: x: 2, y: 2, z: 4, core: 2. Of those that a mesh axis runs over, the one named last changes fastest.
Arguments:
- spectra: bfloat16 [2, 8, 192, 2048], P(None, None, 'src', 'rcv'), as said below
- alive: int32 [192, 2048], P('src', 'rcv'), may hold values 0 or 1
Outputs:
- stacked: bfloat16 [2, 8, 2048, 2048], P(None, None, 'src', 'rcv')
The draws below stay inside these ranges and needn't reach their ends.
Inputs may be any that keep to these rules, and one draw needn't show every extreme that they name: spectra: every entry is a random factor times an amplitude of its window and channel that spreads over a factor of 15.
All inputs are finite; a program needn't handle non-finite values. No bound on the sum of `alive` on one device may be relied on, other than what follows from the above.
Results may differ from the reference program's by a relative error of at most 0.0057.
Values may be sent and summed in bfloat16 or wider, within the bound.
A program may use at most 64 MiB of HBM per device.

```python
import math
import jax
import jax.numpy as jnp
from jax import lax

BINS = 8
WINDOWS = 192
CHANNELS = 2048


def draw_spectra(key, part):
    key_amp = jax.random.fold_in(key, 11)
    key_base = jax.random.fold_in(key, 23)
    amplitude = jnp.exp(jax.random.uniform(key_amp, (1, 1, WINDOWS, CHANNELS), jnp.float32, math.log(0.2), math.log(3.0)))
    base = jax.random.normal(key_base, (2, BINS, WINDOWS, CHANNELS), jnp.float32)
    return (base * amplitude).astype(jnp.bfloat16)


def set_ends(entries, stream_key, least, largest):
    index_at = [jax.random.randint(jax.random.fold_in(stream_key, axis), (), 0, length) for axis, length in enumerate(entries.shape)]
    main_axis = entries.shape.index(max(entries.shape))
    neighbour = index_at[:main_axis] + [(index_at[main_axis] + 1) % entries.shape[main_axis]] + index_at[main_axis + 1:]
    return entries.at[tuple(index_at)].set(least).at[tuple(neighbour)].set(largest)


def setup_inputs(seed: int = 0) -> dict:
    streams_of = jax.random.split(jax.random.key(seed), 3)
    spectra = draw_spectra(jax.random.fold_in(streams_of[2], 71), 0)
    alive = set_ends((jax.random.randint(streams_of[1], (WINDOWS, CHANNELS), 0, 8) < 7).astype(jnp.int32), jax.random.fold_in(streams_of[1], 1), 0, 1)
    return dict(spectra=spectra, alive=alive)


def whiten(spectra, alive):
    values = spectra.astype(jnp.float32)
    power = lax.optimization_barrier(jnp.sum(values * values, axis=(0, 1))) / BINS
    factor = alive.astype(jnp.float32) / jnp.sqrt(jnp.maximum(power, 0.5))
    return (values * factor).astype(jnp.bfloat16)

def one_bin(pair):
    real_part = pair[0]
    imag_part = pair[1]
    first = jnp.dot(real_part.T, real_part, preferred_element_type=jnp.float32)
    second = jnp.dot(imag_part.T, imag_part, preferred_element_type=jnp.float32)
    third = jnp.dot(real_part.T, imag_part, preferred_element_type=jnp.float32)
    fourth = jnp.dot(imag_part.T, real_part, preferred_element_type=jnp.float32)
    return (first + second, third - fourth)

def reference(spectra, alive):
    whitened = whiten(spectra, alive)
    by_bin = jnp.moveaxis(whitened, 1, 0)
    real_stack, imag_stack = lax.map(one_bin, by_bin)
    factor = jnp.float32(1.0) / jnp.sqrt(jnp.float32(WINDOWS))
    return (jnp.stack((real_stack, imag_stack)) * factor).astype(jnp.bfloat16)
```

```python
import functools

import jax
import jax.numpy as jnp
from jax import lax
from jax.experimental import pallas as pl
from jax.experimental.pallas import tpu as pltpu
from jax.sharding import PartitionSpec as P

MESH = pl.DeviceIdType.MESH

N_VIA_X = 0
N_Y_ONCE = 0


def spread(block, axis, holder):
    block = jnp.where(lax.axis_index(axis) == holder, block, jnp.zeros_like(block))
    return lax.psum(block, axis)


def whiten(spectra, alive, bins):
    values = spectra.astype(jnp.float32)
    power = jnp.sum(values * values, axis=(0, 1)) / bins
    factor = alive.astype(jnp.float32) / jnp.sqrt(jnp.maximum(power, 0.5))
    return (values * factor).astype(jnp.bfloat16)


def cross_terms(source_part, receiver_part):
    swapped = jnp.stack((receiver_part[1], -receiver_part[0]))
    real_sum = jnp.einsum(
        "kfwc,kfwd->fcd", source_part, receiver_part, preferred_element_type=jnp.float32
    )
    imag_sum = jnp.einsum(
        "kfwc,kfwd->fcd", source_part, swapped, preferred_element_type=jnp.float32
    )
    return jnp.stack((real_sum, imag_sum))


def general_body(spectra, alive):
    bins = spectra.shape[1]
    whitened = whiten(spectra, alive, bins)
    ratio = lax.axis_size("rcv") // lax.axis_size("src")
    row_index = lax.axis_index("src")
    receivers = lax.all_gather(whitened, "src", axis=2, tiled=True)
    blocks = []
    for offset in range(ratio):
        blocks.append(spread(receivers, "rcv", row_index * ratio + offset))
    sources = jnp.concatenate(blocks, axis=3)
    stacked = cross_terms(sources, receivers)
    total_windows = receivers.shape[2]
    factor = jnp.float32(1.0) / jnp.sqrt(jnp.float32(total_windows))
    return (stacked * factor).astype(jnp.bfloat16)


def kernel(
    n_z,
    spectra_ref,
    alive_ref,
    out_ref,
    col,
    srcs,
    rhs,
    stage,
    r_sib,
    r_x,
    r_fwd,
    r_own,
    r_oth,
    s_sib,
    s_x,
    s_fwd,
    s_up,
    s_dn,
    s_y,
    o_sem,
):
    bins, windows, channels = spectra_ref.shape[1:]
    s = lax.axis_index("src")
    r = lax.axis_index("rcv")
    y = lax.rem(r, 2)
    z = r // 2
    sib = s + 1 - 2 * lax.rem(s, 2)
    xp = lax.rem(s + 2, 4)
    diag = lax.rem(sib + 2, 4)
    ry = r + 1 - 2 * y
    oy = 1 - y
    is_root = z == s
    up_ok = jnp.logical_and(z >= s, z < n_z - 1)
    dn_ok = jnp.logical_and(z <= s, z > 0)

    barrier = pltpu.get_barrier_semaphore()
    for target in ((sib, r), (xp, r), (s, ry)):
        pl.semaphore_signal(barrier, inc=1, device_id=target, device_id_type=MESH)

    @pl.when(z < n_z - 1)
    def _():
        pl.semaphore_signal(barrier, inc=1, device_id=(s, r + 2), device_id_type=MESH)

    @pl.when(z > 0)
    def _():
        pl.semaphore_signal(barrier, inc=1, device_id=(s, r - 2), device_id_type=MESH)

    power = jnp.zeros((windows, channels), jnp.float32)
    for part in range(2):
        for f in range(bins):
            v = spectra_ref[part, f].astype(jnp.float32)
            power = power + v * v
    power = power / bins
    factor = alive_ref[...].astype(jnp.float32) / jnp.sqrt(jnp.maximum(power, 0.5))

    peers = 3 + jnp.where(z < n_z - 1, 1, 0) + jnp.where(z > 0, 1, 0)
    pl.semaphore_wait(barrier, peers)

    def remote(src, dst, send, recv, target):
        return pltpu.make_async_remote_copy(
            src_ref=src,
            dst_ref=dst,
            send_sem=send,
            recv_sem=recv,
            device_id=target,
            device_id_type=MESH,
        )

    def to_sib(f):
        return remote(col.at[f, s], col.at[f, s], s_sib.at[f], r_sib.at[f], (sib, r))

    def to_x(f):
        return remote(col.at[f, s], col.at[f, s], s_x.at[f], r_x.at[f], (xp, r))

    def fwd(f):
        return remote(col.at[f, xp], col.at[f, xp], s_fwd.at[f], r_fwd.at[f], (sib, r))

    def to_up(f):
        return remote(srcs.at[y, f], srcs.at[y, f], s_up.at[f], r_own.at[f], (s, r + 2))

    def to_dn(f):
        return remote(srcs.at[y, f], srcs.at[y, f], s_dn.at[f], r_own.at[f], (s, r - 2))

    def to_y(f):
        return remote(srcs.at[y, f], srcs.at[y, f], s_y.at[f], r_oth.at[f], (s, ry))

    def arrived(ref, sem):
        remote(ref, ref, sem, sem, (sib, r)).wait_recv()

    def put(f, half):
        rows = pl.ds(pl.multiple_of(half * channels, channels), channels)
        return pltpu.make_async_copy(
            stage.at[f, half], out_ref.at[:, f, rows, :], o_sem.at[f, half]
        )

    for f in range(bins):
        for part in range(2):
            v = spectra_ref[part, f].astype(jnp.float32)
            col[f, s, part] = (v * factor).astype(jnp.bfloat16)
        to_x(f).start()
        to_sib(f).start()

    n_src = col.shape[1]
    depth = n_src * 2 * windows
    scale = jnp.float32(1.0) / jnp.sqrt(jnp.float32(n_src * windows))

    def multiply(f, half):
        left = srcs[half, f].reshape(depth, channels)
        acc = lax.dot_general(
            left,
            rhs[...].reshape(depth, 2 * channels),
            (((0,), (0,)), ((), ())),
            preferred_element_type=jnp.float32,
        )
        acc = (acc * scale).astype(jnp.bfloat16)
        stage[f, half, 0] = acc[:, :channels]
        stage[f, half, 1] = acc[:, channels:]
        put(f, half).start()

    def step(f, carry):
        @pl.when(f < bins)
        def _():
            arrived(col.at[f, xp], r_x.at[f])
            fwd(f).start()
            arrived(col.at[f, sib], r_sib.at[f])
            arrived(col.at[f, diag], r_fwd.at[f])

            @pl.when(is_root)
            def _():
                srcs[y, f] = col[f]

            @pl.when(jnp.logical_not(is_root))
            def _():
                arrived(srcs.at[y, f], r_own.at[f])

            @pl.when(up_ok)
            def _():
                to_up(f).start()

            @pl.when(dn_ok)
            def _():
                to_dn(f).start()

            to_y(f).start()

        @pl.when(f >= 1)
        def _():
            g = f - 1
            whole = col[g]
            rhs[:, :, :, :channels] = whole
            rhs[:, 0, :, channels:] = whole[:, 1]
            rhs[:, 1, :, channels:] = -whole[:, 0]
            multiply(g, y)
            arrived(srcs.at[oy, g], r_oth.at[g])
            multiply(g, oy)

        return carry

    lax.fori_loop(0, bins + 1, step, 0)

    def drain(f, carry):
        to_sib(f).wait_send()
        to_x(f).wait_send()
        fwd(f).wait_send()
        to_y(f).wait_send()

        @pl.when(up_ok)
        def _():
            to_up(f).wait_send()

        @pl.when(dn_ok)
        def _():
            to_dn(f).wait_send()

        put(f, 0).wait()
        put(f, 1).wait()
        return carry

    lax.fori_loop(0, bins, drain, 0)


def grid_body(n_z, spectra, alive):
    parts, bins, windows, channels = spectra.shape
    n_src = lax.axis_size("src")
    dma = pltpu.SemaphoreType.DMA
    rows = 2 * channels
    return pl.pallas_call(
        functools.partial(kernel, n_z),
        out_shape=jax.ShapeDtypeStruct((parts, bins, rows, channels), jnp.bfloat16),
        in_specs=[pl.BlockSpec(memory_space=pltpu.VMEM)] * 2,
        out_specs=pl.BlockSpec(memory_space=pl.ANY),
        scratch_shapes=[
            pltpu.VMEM((bins, n_src, parts, windows, channels), jnp.bfloat16),
            pltpu.VMEM((2, bins, n_src, parts, windows, channels), jnp.bfloat16),
            pltpu.VMEM((n_src, parts, windows, 2 * channels), jnp.bfloat16),
            pltpu.VMEM((bins, 2, parts, channels, channels), jnp.bfloat16),
        ]
        + [dma((bins,))] * 11
        + [dma((bins, 2))],
        compiler_params=pltpu.CompilerParams(
            collective_id=0, has_side_effects=True, vmem_limit_bytes=48 * 2**20
        ),
        cost_estimate=pl.CostEstimate(
            flops=8 * bins * n_src * windows * rows * channels,
            bytes_accessed=10 * spectra.size * parts * n_src,
            transcendentals=0,
        ),
    )(spectra, alive)


def solution(mesh):
    if mesh.shape["src"] == 4 and mesh.shape["rcv"] == 8:
        body = functools.partial(grid_body, mesh.shape["rcv"] // 2)
    else:
        body = general_body
    return jax.shard_map(
        body,
        mesh=mesh,
        in_specs=(P(None, None, "src", "rcv"), P("src", "rcv")),
        out_specs=P(None, None, "src", "rcv"),
        check_vma=False,
    )
```

```python
import functools

import jax
import jax.numpy as jnp
from jax import lax
from jax.experimental import pallas as pl
from jax.experimental.pallas import tpu as pltpu
from jax.sharding import PartitionSpec as P

MESH = pl.DeviceIdType.MESH

N_Y_ONCE = 2


def spread(block, axis, holder):
    block = jnp.where(lax.axis_index(axis) == holder, block, jnp.zeros_like(block))
    return lax.psum(block, axis)


def whiten(spectra, alive, bins):
    values = spectra.astype(jnp.float32)
    power = jnp.sum(values * values, axis=(0, 1)) / bins
    factor = alive.astype(jnp.float32) / jnp.sqrt(jnp.maximum(power, 0.5))
    return (values * factor).astype(jnp.bfloat16)


def cross_terms(source_part, receiver_part):
    swapped = jnp.stack((receiver_part[1], -receiver_part[0]))
    real_sum = jnp.einsum(
        "kfwc,kfwd->fcd", source_part, receiver_part, preferred_element_type=jnp.float32
    )
    imag_sum = jnp.einsum(
        "kfwc,kfwd->fcd", source_part, swapped, preferred_element_type=jnp.float32
    )
    return jnp.stack((real_sum, imag_sum))


def general_body(spectra, alive):
    bins = spectra.shape[1]
    whitened = whiten(spectra, alive, bins)
    ratio = lax.axis_size("rcv") // lax.axis_size("src")
    row_index = lax.axis_index("src")
    receivers = lax.all_gather(whitened, "src", axis=2, tiled=True)
    blocks = []
    for offset in range(ratio):
        blocks.append(spread(receivers, "rcv", row_index * ratio + offset))
    sources = jnp.concatenate(blocks, axis=3)
    stacked = cross_terms(sources, receivers)
    total_windows = receivers.shape[2]
    factor = jnp.float32(1.0) / jnp.sqrt(jnp.float32(total_windows))
    return (stacked * factor).astype(jnp.bfloat16)


def kernel(
    n_z,
    spectra_hbm,
    alive_hbm,
    out_ref,
    spectra_ref,
    alive_ref,
    col,
    srcs,
    transit,
    rhs,
    stage,
    r_sib,
    r_x,
    r_fwd,
    r_z,
    r_t,
    r_tx,
    r_ya,
    r_yb,
    s_sib,
    s_x,
    s_fwd,
    s_up,
    s_dn,
    s_tup,
    s_tdn,
    s_tx,
    s_ya,
    s_yb,
    s_up2,
    s_dn2,
    i_sem,
    o_sem,
):
    bins, windows, channels = spectra_ref.shape[1:]
    s = lax.axis_index("src")
    r = lax.axis_index("rcv")
    x = s // 2
    core = lax.rem(s, 2)
    y = lax.rem(r, 2)
    z = r // 2
    ox, ocore, oy = 1 - x, 1 - core, 1 - y
    sib = 2 * x + ocore
    xp = 2 * ox + core
    ry = r + 1 - 2 * y
    is_root = z == s
    is_troot = z == xp
    up_ok = jnp.logical_and(z >= s, z < n_z - 1)
    dn_ok = jnp.logical_and(z <= s, z > 0)
    tup_ok = jnp.logical_and(z >= xp, z < n_z - 1)
    tdn_ok = jnp.logical_and(z <= xp, z > 0)

    load_spectra = pltpu.make_async_copy(spectra_hbm, spectra_ref, i_sem.at[0])
    load_alive = pltpu.make_async_copy(alive_hbm, alive_ref, i_sem.at[1])
    load_spectra.start()
    load_alive.start()

    barrier = pltpu.get_barrier_semaphore()
    for target in ((sib, r), (xp, r), (s, ry)):
        pl.semaphore_signal(barrier, inc=1, device_id=target, device_id_type=MESH)

    @pl.when(z < n_z - 1)
    def _():
        pl.semaphore_signal(barrier, inc=1, device_id=(s, r + 2), device_id_type=MESH)

    @pl.when(z > 0)
    def _():
        pl.semaphore_signal(barrier, inc=1, device_id=(s, r - 2), device_id_type=MESH)

    load_spectra.wait()
    load_alive.wait()
    power = jnp.zeros((windows, channels), jnp.float32)
    for part in range(2):
        for f in range(bins):
            v = spectra_ref[part, f].astype(jnp.float32)
            power = power + v * v
    power = power / bins
    factor = alive_ref[...].astype(jnp.float32) / jnp.sqrt(jnp.maximum(power, 0.5))

    peers = 3 + jnp.where(z < n_z - 1, 1, 0) + jnp.where(z > 0, 1, 0)
    pl.semaphore_wait(barrier, peers)

    def remote(src, dst, send, recv, target):
        return pltpu.make_async_remote_copy(
            src_ref=src,
            dst_ref=dst,
            send_sem=send,
            recv_sem=recv,
            device_id=target,
            device_id_type=MESH,
        )

    above, below, across = (s, r + 2), (s, r - 2), (s, ry)

    def to_sib(f):
        block = col.at[f, x, core]
        return remote(block, block, s_sib.at[f], r_sib.at[f], (sib, r))

    def to_x(f):
        block = col.at[f, x, core]
        return remote(block, block, s_x.at[f], r_x.at[f], (xp, r))

    def fwd(f):
        block = col.at[f, ox, core]
        return remote(block, block, s_fwd.at[f], r_fwd.at[f], (sib, r))

    def to_up(f):
        block = srcs.at[y, f, x]
        return remote(block, block, s_up.at[f], r_z.at[f], above)

    def to_dn(f):
        block = srcs.at[y, f, x]
        return remote(block, block, s_dn.at[f], r_z.at[f], below)

    def to_ya(f):
        block = srcs.at[y, f, x]
        return remote(block, block, s_ya.at[f], r_ya.at[f], across)

    def to_yb(f):
        block = srcs.at[y, f, ox]
        return remote(block, block, s_yb.at[f], r_yb.at[f], across)

    def to_up2(f):
        block = srcs.at[oy, f, x]
        return remote(block, block, s_up2.at[f], r_ya.at[f], above)

    def to_dn2(f):
        block = srcs.at[oy, f, x]
        return remote(block, block, s_dn2.at[f], r_ya.at[f], below)

    def to_tup(f):
        return remote(transit.at[f], transit.at[f], s_tup.at[f], r_t.at[f], above)

    def to_tdn(f):
        return remote(transit.at[f], transit.at[f], s_tdn.at[f], r_t.at[f], below)

    def to_tx(f):
        block = srcs.at[y, f, x]
        return remote(transit.at[f], block, s_tx.at[f], r_tx.at[f], (xp, r))

    def arrived(ref, sem):
        remote(ref, ref, sem, sem, (sib, r)).wait_recv()

    def put(f, half):
        rows = pl.ds(pl.multiple_of(half * channels, channels), channels)
        return pltpu.make_async_copy(
            stage.at[f, half], out_ref.at[:, f, rows, :], o_sem.at[f, half]
        )

    for f in range(bins):
        for part in range(2):
            v = spectra_ref[part, f].astype(jnp.float32)
            col[f, x, core, part] = (v * factor).astype(jnp.bfloat16)
        to_sib(f).start()
        to_x(f).start()

    n_src = col.shape[1] * col.shape[2]
    depth = n_src * 2 * windows
    scale = jnp.float32(1.0) / jnp.sqrt(jnp.float32(n_src * windows))

    def multiply(f, half):
        acc = lax.dot_general(
            srcs[half, f].reshape(depth, channels),
            rhs[...].reshape(depth, 2 * channels),
            (((0,), (0,)), ((), ())),
            preferred_element_type=jnp.float32,
        )
        acc = (acc * scale).astype(jnp.bfloat16)
        stage[f, half, 0] = acc[:, :channels]
        stage[f, half, 1] = acc[:, channels:]
        put(f, half).start()

    def both(first, second):
        return jnp.logical_and(first, second)

    def send_along(f):
        arrived(col.at[f, x, ocore], r_sib.at[f])

        @pl.when(is_root)
        def _():
            srcs[y, f, x] = col[f, x]

        @pl.when(jnp.logical_not(is_root))
        def _():
            arrived(srcs.at[y, f, x], r_z.at[f])

        @pl.when(up_ok)
        def _():
            to_up(f).start()

        @pl.when(dn_ok)
        def _():
            to_dn(f).start()

        @pl.when(jnp.logical_or(is_root, f >= N_Y_ONCE))
        def _():
            to_ya(f).start()

        @pl.when(is_troot)
        def _():
            transit[f] = col[f, x]

        @pl.when(jnp.logical_not(is_troot))
        def _():
            arrived(transit.at[f], r_t.at[f])

        @pl.when(tup_ok)
        def _():
            to_tup(f).start()

        @pl.when(tdn_ok)
        def _():
            to_tdn(f).start()

        @pl.when(jnp.logical_not(is_troot))
        def _():
            to_tx(f).start()

        arrived(col.at[f, ox, core], r_x.at[f])
        fwd(f).start()

    def send_across(f):
        arrived(col.at[f, ox, ocore], r_fwd.at[f])

        @pl.when(is_root)
        def _():
            srcs[y, f, ox] = col[f, ox]

        @pl.when(jnp.logical_not(is_root))
        def _():
            arrived(srcs.at[y, f, ox], r_tx.at[f])

        to_yb(f).start()
        arrived(srcs.at[oy, f, x], r_ya.at[f])

        @pl.when(both(up_ok, f < N_Y_ONCE))
        def _():
            to_up2(f).start()

        @pl.when(both(dn_ok, f < N_Y_ONCE))
        def _():
            to_dn2(f).start()

    def finish(f):
        whole = col[f]
        rhs[:, :, :, :, :channels] = whole
        rhs[:, :, 0, :, channels:] = whole[:, :, 1]
        rhs[:, :, 1, :, channels:] = -whole[:, :, 0]
        multiply(f, y)
        arrived(srcs.at[oy, f, ox], r_yb.at[f])
        multiply(f, oy)

    def step(f, carry):
        @pl.when(f < bins)
        def _():
            send_along(f)

        @pl.when(both(f >= 1, f < bins + 1))
        def _():
            send_across(f - 1)

        @pl.when(f >= 2)
        def _():
            finish(f - 2)

        return carry

    lax.fori_loop(0, bins + 2, step, 0)

    def drain(f, carry):
        to_sib(f).wait_send()
        to_x(f).wait_send()
        fwd(f).wait_send()
        to_yb(f).wait_send()

        for sent, condition in (
            (to_up, up_ok),
            (to_dn, dn_ok),
            (to_ya, jnp.logical_or(is_root, f >= N_Y_ONCE)),
            (to_tup, tup_ok),
            (to_tdn, tdn_ok),
            (to_tx, jnp.logical_not(is_troot)),
            (to_up2, both(up_ok, f < N_Y_ONCE)),
            (to_dn2, both(dn_ok, f < N_Y_ONCE)),
        ):

            @pl.when(condition)
            def _(sent=sent):
                sent(f).wait_send()

        put(f, 0).wait()
        put(f, 1).wait()
        return carry

    lax.fori_loop(0, bins, drain, 0)


def grid_body(n_z, spectra, alive):
    parts, bins, windows, channels = spectra.shape
    n_src = lax.axis_size("src")
    dma = pltpu.SemaphoreType.DMA
    rows = 2 * channels
    block = (2, parts, windows, channels)
    return pl.pallas_call(
        functools.partial(kernel, n_z),
        out_shape=jax.ShapeDtypeStruct((parts, bins, rows, channels), jnp.bfloat16),
        in_specs=[pl.BlockSpec(memory_space=pl.ANY)] * 2,
        out_specs=pl.BlockSpec(memory_space=pl.ANY),
        scratch_shapes=[
            pltpu.VMEM(spectra.shape, jnp.bfloat16),
            pltpu.VMEM(alive.shape, jnp.int32),
            pltpu.VMEM((bins, 2) + block, jnp.bfloat16),
            pltpu.VMEM((2, bins, 2) + block, jnp.bfloat16),
            pltpu.VMEM((bins,) + block, jnp.bfloat16),
            pltpu.VMEM((2, 2, parts, windows, 2 * channels), jnp.bfloat16),
            pltpu.VMEM((bins, 2, parts, channels, channels), jnp.bfloat16),
        ]
        + [dma((bins,))] * 20
        + [dma((2,)), dma((bins, 2))],
        compiler_params=pltpu.CompilerParams(
            collective_id=0, has_side_effects=True, vmem_limit_bytes=48 * 2**20
        ),
        cost_estimate=pl.CostEstimate(
            flops=8 * bins * n_src * windows * rows * channels,
            bytes_accessed=10 * spectra.size * parts * n_src,
            transcendentals=0,
        ),
    )(spectra, alive)


def solution(mesh):
    if mesh.shape["src"] == 4 and mesh.shape["rcv"] == 8:
        body = functools.partial(grid_body, mesh.shape["rcv"] // 2)
    else:
        body = general_body
    return jax.shard_map(
        body,
        mesh=mesh,
        in_specs=(P(None, None, "src", "rcv"), P("src", "rcv")),
        out_specs=P(None, None, "src", "rcv"),
        check_vma=False,
    )
```

```python
import functools

import jax
import jax.numpy as jnp
from jax import lax
from jax.experimental import pallas as pl
from jax.experimental.pallas import tpu as pltpu
from jax.sharding import PartitionSpec as P

MESH = pl.DeviceIdType.MESH

N_Y_ONCE = 2
HOP = 2


def spread(block, axis, holder):
    block = jnp.where(lax.axis_index(axis) == holder, block, jnp.zeros_like(block))
    return lax.psum(block, axis)


def whiten(spectra, alive, bins):
    values = spectra.astype(jnp.float32)
    power = jnp.sum(values * values, axis=(0, 1)) / bins
    factor = alive.astype(jnp.float32) / jnp.sqrt(jnp.maximum(power, 0.5))
    return (values * factor).astype(jnp.bfloat16)


def cross_terms(source_part, receiver_part):
    swapped = jnp.stack((receiver_part[1], -receiver_part[0]))
    real_sum = jnp.einsum(
        "kfwc,kfwd->fcd", source_part, receiver_part, preferred_element_type=jnp.float32
    )
    imag_sum = jnp.einsum(
        "kfwc,kfwd->fcd", source_part, swapped, preferred_element_type=jnp.float32
    )
    return jnp.stack((real_sum, imag_sum))


def general_body(spectra, alive):
    bins = spectra.shape[1]
    whitened = whiten(spectra, alive, bins)
    ratio = lax.axis_size("rcv") // lax.axis_size("src")
    row_index = lax.axis_index("src")
    receivers = lax.all_gather(whitened, "src", axis=2, tiled=True)
    blocks = []
    for offset in range(ratio):
        blocks.append(spread(receivers, "rcv", row_index * ratio + offset))
    sources = jnp.concatenate(blocks, axis=3)
    stacked = cross_terms(sources, receivers)
    total_windows = receivers.shape[2]
    factor = jnp.float32(1.0) / jnp.sqrt(jnp.float32(total_windows))
    return (stacked * factor).astype(jnp.bfloat16)


def kernel(
    n_z,
    spectra_hbm,
    alive_hbm,
    out_ref,
    spectra_ref,
    alive_ref,
    col,
    srcs,
    transit,
    rhs,
    stage,
    r_sib,
    r_x,
    r_fwd,
    r_z,
    r_t,
    r_tx,
    r_ya,
    r_yb,
    s_sib,
    s_x,
    s_fwd,
    s_up,
    s_dn,
    s_tup,
    s_tdn,
    s_tx,
    s_ya,
    s_yb,
    s_up2,
    s_dn2,
    i_sem,
    o_sem,
):
    bins, windows, channels = spectra_ref.shape[1:]
    s = lax.axis_index("src")
    r = lax.axis_index("rcv")
    x = s // 2
    core = lax.rem(s, 2)
    y = lax.rem(r, 2)
    z = r // 2
    ox, ocore, oy = 1 - x, 1 - core, 1 - y
    sib = 2 * x + ocore
    xp = 2 * ox + core
    ry = r + 1 - 2 * y
    is_root = z == s
    is_troot = z == xp
    up_ok = jnp.logical_and(z >= s, z < n_z - 1)
    dn_ok = jnp.logical_and(z <= s, z > 0)
    tup_ok = jnp.logical_and(z >= xp, z < n_z - 1)
    tdn_ok = jnp.logical_and(z <= xp, z > 0)

    load_spectra = pltpu.make_async_copy(spectra_hbm, spectra_ref, i_sem.at[0])
    load_alive = pltpu.make_async_copy(alive_hbm, alive_ref, i_sem.at[1])
    load_spectra.start()
    load_alive.start()

    barrier = pltpu.get_barrier_semaphore()
    for target in ((sib, r), (xp, r), (s, ry)):
        pl.semaphore_signal(barrier, inc=1, device_id=target, device_id_type=MESH)

    @pl.when(z < n_z - 1)
    def _():
        pl.semaphore_signal(barrier, inc=1, device_id=(s, r + 2), device_id_type=MESH)

    @pl.when(z > 0)
    def _():
        pl.semaphore_signal(barrier, inc=1, device_id=(s, r - 2), device_id_type=MESH)

    load_spectra.wait()
    load_alive.wait()
    power = jnp.zeros((windows, channels), jnp.float32)
    for part in range(2):
        for f in range(bins):
            v = spectra_ref[part, f].astype(jnp.float32)
            power = power + v * v
    power = power / bins
    factor = alive_ref[...].astype(jnp.float32) / jnp.sqrt(jnp.maximum(power, 0.5))

    peers = 3 + jnp.where(z < n_z - 1, 1, 0) + jnp.where(z > 0, 1, 0)
    pl.semaphore_wait(barrier, peers)

    def remote(src, dst, send, recv, target):
        return pltpu.make_async_remote_copy(
            src_ref=src,
            dst_ref=dst,
            send_sem=send,
            recv_sem=recv,
            device_id=target,
            device_id_type=MESH,
        )

    above, below, across = (s, r + 2), (s, r - 2), (s, ry)

    def to_sib(f):
        block = col.at[f, x, core]
        return remote(block, block, s_sib.at[f], r_sib.at[f], (sib, r))

    def to_x(f):
        block = col.at[f, x, core]
        return remote(block, block, s_x.at[f], r_x.at[f], (xp, r))

    def fwd(f):
        block = col.at[f, ox, core]
        return remote(block, block, s_fwd.at[f], r_fwd.at[f], (sib, r))

    def to_up(f):
        block = srcs.at[y, f, x]
        return remote(block, block, s_up.at[f], r_z.at[f], above)

    def to_dn(f):
        block = srcs.at[y, f, x]
        return remote(block, block, s_dn.at[f], r_z.at[f], below)

    def to_ya(f):
        block = srcs.at[y, f, x]
        return remote(block, block, s_ya.at[f], r_ya.at[f], across)

    def to_yb(f):
        block = srcs.at[y, f, ox]
        return remote(block, block, s_yb.at[f], r_yb.at[f], across)

    def to_up2(f):
        block = srcs.at[oy, f, x]
        return remote(block, block, s_up2.at[f], r_ya.at[f], above)

    def to_dn2(f):
        block = srcs.at[oy, f, x]
        return remote(block, block, s_dn2.at[f], r_ya.at[f], below)

    def to_tup(f):
        return remote(transit.at[f], transit.at[f], s_tup.at[f], r_t.at[f], above)

    def to_tdn(f):
        return remote(transit.at[f], transit.at[f], s_tdn.at[f], r_t.at[f], below)

    def to_tx(f):
        block = srcs.at[y, f, x]
        return remote(transit.at[f], block, s_tx.at[f], r_tx.at[f], (xp, r))

    def arrived(ref, sem):
        remote(ref, ref, sem, sem, (sib, r)).wait_recv()

    def put(f, half):
        rows = pl.ds(pl.multiple_of(half * channels, channels), channels)
        return pltpu.make_async_copy(
            stage.at[f, half], out_ref.at[:, f, rows, :], o_sem.at[f, half]
        )

    for f in range(bins):
        for part in range(2):
            v = spectra_ref[part, f].astype(jnp.float32)
            col[f, x, core, part] = (v * factor).astype(jnp.bfloat16)
        to_sib(f).start()
        to_x(f).start()

    n_src = col.shape[1] * col.shape[2]
    depth = n_src * 2 * windows
    scale = jnp.float32(1.0) / jnp.sqrt(jnp.float32(n_src * windows))

    def multiply(f, half):
        acc = lax.dot_general(
            srcs[half, f].reshape(depth, channels),
            rhs[...].reshape(depth, 2 * channels),
            (((0,), (0,)), ((), ())),
            preferred_element_type=jnp.float32,
        )
        acc = (acc * scale).astype(jnp.bfloat16)
        stage[f, half, 0] = acc[:, :channels]
        stage[f, half, 1] = acc[:, channels:]
        put(f, half).start()

    def both(first, second):
        return jnp.logical_and(first, second)

    def along_own(f):
        @pl.when(is_root)
        def _():
            arrived(col.at[f, x, ocore], r_sib.at[f])
            srcs[y, f, x] = col[f, x]

        @pl.when(jnp.logical_not(is_root))
        def _():
            arrived(srcs.at[y, f, x], r_z.at[f])

        @pl.when(up_ok)
        def _():
            to_up(f).start()

        @pl.when(dn_ok)
        def _():
            to_dn(f).start()

        @pl.when(jnp.logical_or(is_root, f >= N_Y_ONCE))
        def _():
            to_ya(f).start()

    def along_transit(f):
        @pl.when(is_troot)
        def _():
            arrived(col.at[f, x, ocore], r_sib.at[f])
            transit[f] = col[f, x]

        @pl.when(jnp.logical_not(is_troot))
        def _():
            arrived(transit.at[f], r_t.at[f])

        @pl.when(tup_ok)
        def _():
            to_tup(f).start()

        @pl.when(tdn_ok)
        def _():
            to_tdn(f).start()

        @pl.when(jnp.logical_not(is_troot))
        def _():
            to_tx(f).start()

    def column(f):
        arrived(col.at[f, ox, core], r_x.at[f])
        fwd(f).start()

    def across_other(f):
        @pl.when(is_root)
        def _():
            arrived(col.at[f, ox, ocore], r_fwd.at[f])
            srcs[y, f, ox] = col[f, ox]

        @pl.when(jnp.logical_not(is_root))
        def _():
            arrived(srcs.at[y, f, ox], r_tx.at[f])

        to_yb(f).start()

    def across_once(f):
        arrived(srcs.at[oy, f, x], r_ya.at[f])

        @pl.when(up_ok)
        def _():
            to_up2(f).start()

        @pl.when(dn_ok)
        def _():
            to_dn2(f).start()

    def finish(f):
        @pl.when(jnp.logical_not(jnp.logical_or(is_root, is_troot)))
        def _():
            arrived(col.at[f, x, ocore], r_sib.at[f])

        @pl.when(jnp.logical_not(is_root))
        def _():
            arrived(col.at[f, ox, ocore], r_fwd.at[f])

        @pl.when(f >= N_Y_ONCE)
        def _():
            arrived(srcs.at[oy, f, x], r_ya.at[f])

        whole = col[f]
        rhs[:, :, :, :, :channels] = whole
        rhs[:, :, 0, :, channels:] = whole[:, :, 1]
        rhs[:, :, 1, :, channels:] = -whole[:, :, 0]
        multiply(f, y)
        arrived(srcs.at[oy, f, ox], r_yb.at[f])
        multiply(f, oy)

    dist = HOP * jnp.where(z > s, z - s, s - z)
    tdist = HOP * jnp.where(z > xp, z - xp, xp - z)
    b_lag = HOP + jnp.where(is_root, HOP, dist)
    last = b_lag + HOP
    n_steps = bins + HOP * (n_z + 1)

    def step(t, carry):
        for work, lag, count in (
            (along_own, dist, bins),
            (along_transit, tdist, bins),
            (column, 1, bins),
            (across_once, dist + HOP, N_Y_ONCE),
            (across_other, b_lag, bins),
            (finish, last, bins),
        ):

            @pl.when(both(t >= lag, t < lag + count))
            def _(work=work, lag=lag):
                work(t - lag)

        return carry

    lax.fori_loop(0, n_steps, step, 0)

    def drain(f, carry):
        to_sib(f).wait_send()
        to_x(f).wait_send()
        fwd(f).wait_send()
        to_yb(f).wait_send()

        for sent, condition in (
            (to_up, up_ok),
            (to_dn, dn_ok),
            (to_ya, jnp.logical_or(is_root, f >= N_Y_ONCE)),
            (to_tup, tup_ok),
            (to_tdn, tdn_ok),
            (to_tx, jnp.logical_not(is_troot)),
            (to_up2, both(up_ok, f < N_Y_ONCE)),
            (to_dn2, both(dn_ok, f < N_Y_ONCE)),
        ):

            @pl.when(condition)
            def _(sent=sent):
                sent(f).wait_send()

        put(f, 0).wait()
        put(f, 1).wait()
        return carry

    lax.fori_loop(0, bins, drain, 0)


def grid_body(n_z, spectra, alive):
    parts, bins, windows, channels = spectra.shape
    n_src = lax.axis_size("src")
    dma = pltpu.SemaphoreType.DMA
    rows = 2 * channels
    block = (2, parts, windows, channels)
    return pl.pallas_call(
        functools.partial(kernel, n_z),
        out_shape=jax.ShapeDtypeStruct((parts, bins, rows, channels), jnp.bfloat16),
        in_specs=[pl.BlockSpec(memory_space=pl.ANY)] * 2,
        out_specs=pl.BlockSpec(memory_space=pl.ANY),
        scratch_shapes=[
            pltpu.VMEM(spectra.shape, jnp.bfloat16),
            pltpu.VMEM(alive.shape, jnp.int32),
            pltpu.VMEM((bins, 2) + block, jnp.bfloat16),
            pltpu.VMEM((2, bins, 2) + block, jnp.bfloat16),
            pltpu.VMEM((bins,) + block, jnp.bfloat16),
            pltpu.VMEM((2, 2, parts, windows, 2 * channels), jnp.bfloat16),
            pltpu.VMEM((bins, 2, parts, channels, channels), jnp.bfloat16),
        ]
        + [dma((bins,))] * 20
        + [dma((2,)), dma((bins, 2))],
        compiler_params=pltpu.CompilerParams(
            collective_id=0, has_side_effects=True, vmem_limit_bytes=48 * 2**20
        ),
        cost_estimate=pl.CostEstimate(
            flops=8 * bins * n_src * windows * rows * channels,
            bytes_accessed=10 * spectra.size * parts * n_src,
            transcendentals=0,
        ),
    )(spectra, alive)


def solution(mesh):
    if mesh.shape["src"] == 4 and mesh.shape["rcv"] == 8:
        body = functools.partial(grid_body, mesh.shape["rcv"] // 2)
    else:
        body = general_body
    return jax.shard_map(
        body,
        mesh=mesh,
        in_specs=(P(None, None, "src", "rcv"), P("src", "rcv")),
        out_specs=P(None, None, "src", "rcv"),
        check_vma=False,
    )
```

```python
import functools

import jax
import jax.numpy as jnp
from jax import lax
from jax.experimental import pallas as pl
from jax.experimental.pallas import tpu as pltpu
from jax.sharding import PartitionSpec as P

MESH = pl.DeviceIdType.MESH

N_Y_ONCE = 4
HOP = 3


def spread(block, axis, holder):
    block = jnp.where(lax.axis_index(axis) == holder, block, jnp.zeros_like(block))
    return lax.psum(block, axis)


def whiten(spectra, alive, bins):
    values = spectra.astype(jnp.float32)
    power = jnp.sum(values * values, axis=(0, 1)) / bins
    factor = alive.astype(jnp.float32) / jnp.sqrt(jnp.maximum(power, 0.5))
    return (values * factor).astype(jnp.bfloat16)


def cross_terms(source_part, receiver_part):
    swapped = jnp.stack((receiver_part[1], -receiver_part[0]))
    real_sum = jnp.einsum(
        "kfwc,kfwd->fcd", source_part, receiver_part, preferred_element_type=jnp.float32
    )
    imag_sum = jnp.einsum(
        "kfwc,kfwd->fcd", source_part, swapped, preferred_element_type=jnp.float32
    )
    return jnp.stack((real_sum, imag_sum))


def general_body(spectra, alive):
    bins = spectra.shape[1]
    whitened = whiten(spectra, alive, bins)
    ratio = lax.axis_size("rcv") // lax.axis_size("src")
    row_index = lax.axis_index("src")
    receivers = lax.all_gather(whitened, "src", axis=2, tiled=True)
    blocks = []
    for offset in range(ratio):
        blocks.append(spread(receivers, "rcv", row_index * ratio + offset))
    sources = jnp.concatenate(blocks, axis=3)
    stacked = cross_terms(sources, receivers)
    total_windows = receivers.shape[2]
    factor = jnp.float32(1.0) / jnp.sqrt(jnp.float32(total_windows))
    return (stacked * factor).astype(jnp.bfloat16)


def kernel(
    n_z,
    spectra_hbm,
    alive_hbm,
    out_ref,
    spectra_ref,
    alive_ref,
    col,
    srcs,
    transit,
    rhs,
    stage,
    r_sib,
    r_x,
    r_fwd,
    r_z,
    r_t,
    r_tx,
    r_ya,
    r_yb,
    s_sib,
    s_x,
    s_fwd,
    s_up,
    s_dn,
    s_tup,
    s_tdn,
    s_tx,
    s_ya,
    s_yb,
    s_up2,
    s_dn2,
    i_sem,
    o_sem,
):
    bins, windows, channels = spectra_ref.shape[1:]
    chunks = 2 * bins
    s = lax.axis_index("src")
    r = lax.axis_index("rcv")
    x = s // 2
    core = lax.rem(s, 2)
    y = lax.rem(r, 2)
    z = r // 2
    ox, ocore, oy = 1 - x, 1 - core, 1 - y
    sib = 2 * x + ocore
    xp = 2 * ox + core
    ry = r + 1 - 2 * y
    is_root = z == s
    is_troot = z == xp
    up_ok = jnp.logical_and(z >= s, z < n_z - 1)
    dn_ok = jnp.logical_and(z <= s, z > 0)
    tup_ok = jnp.logical_and(z >= xp, z < n_z - 1)
    tdn_ok = jnp.logical_and(z <= xp, z > 0)

    load_spectra = pltpu.make_async_copy(spectra_hbm, spectra_ref, i_sem.at[0])
    load_alive = pltpu.make_async_copy(alive_hbm, alive_ref, i_sem.at[1])
    load_spectra.start()
    load_alive.start()

    barrier = pltpu.get_barrier_semaphore()
    for target in ((sib, r), (xp, r), (s, ry)):
        pl.semaphore_signal(barrier, inc=1, device_id=target, device_id_type=MESH)

    @pl.when(z < n_z - 1)
    def _():
        pl.semaphore_signal(barrier, inc=1, device_id=(s, r + 2), device_id_type=MESH)

    @pl.when(z > 0)
    def _():
        pl.semaphore_signal(barrier, inc=1, device_id=(s, r - 2), device_id_type=MESH)

    load_spectra.wait()
    load_alive.wait()
    power = jnp.zeros((windows, channels), jnp.float32)
    for part in range(2):
        for f in range(bins):
            v = spectra_ref[part, f].astype(jnp.float32)
            power = power + v * v
    power = power / bins
    factor = alive_ref[...].astype(jnp.float32) / jnp.sqrt(jnp.maximum(power, 0.5))

    peers = 3 + jnp.where(z < n_z - 1, 1, 0) + jnp.where(z > 0, 1, 0)
    pl.semaphore_wait(barrier, peers)

    def remote(src, dst, send, recv, target):
        return pltpu.make_async_remote_copy(
            src_ref=src,
            dst_ref=dst,
            send_sem=send,
            recv_sem=recv,
            device_id=target,
            device_id_type=MESH,
        )

    above, below, across = (s, r + 2), (s, r - 2), (s, ry)

    def to_sib(f):
        block = col.at[f, x, core]
        return remote(block, block, s_sib.at[f], r_sib.at[f], (sib, r))

    def to_x(f):
        block = col.at[f, x, core]
        return remote(block, block, s_x.at[f], r_x.at[f], (xp, r))

    def fwd(f):
        block = col.at[f, ox, core]
        return remote(block, block, s_fwd.at[f], r_fwd.at[f], (sib, r))

    def to_up(f):
        block = srcs.at[y, f, x]
        return remote(block, block, s_up.at[f], r_z.at[f], above)

    def to_dn(f):
        block = srcs.at[y, f, x]
        return remote(block, block, s_dn.at[f], r_z.at[f], below)

    def to_ya(f):
        block = srcs.at[y, f, x]
        return remote(block, block, s_ya.at[f], r_ya.at[f], across)

    def to_yb(f):
        block = srcs.at[y, f, ox]
        return remote(block, block, s_yb.at[f], r_yb.at[f], across)

    def to_up2(f):
        block = srcs.at[oy, f, x]
        return remote(block, block, s_up2.at[f], r_ya.at[f], above)

    def to_dn2(f):
        block = srcs.at[oy, f, x]
        return remote(block, block, s_dn2.at[f], r_ya.at[f], below)

    def to_tup(f):
        return remote(transit.at[f], transit.at[f], s_tup.at[f], r_t.at[f], above)

    def to_tdn(f):
        return remote(transit.at[f], transit.at[f], s_tdn.at[f], r_t.at[f], below)

    def to_tx(f):
        block = srcs.at[y, f, x]
        return remote(transit.at[f], block, s_tx.at[f], r_tx.at[f], (xp, r))

    def arrived(ref, sem):
        remote(ref, ref, sem, sem, (sib, r)).wait_recv()

    def put(f, half):
        rows = pl.ds(pl.multiple_of(half * channels, channels), channels)
        return pltpu.make_async_copy(
            stage.at[f, half], out_ref.at[:, f, rows, :], o_sem.at[f, half]
        )

    for f in range(bins):
        for part in range(2):
            v = spectra_ref[part, f].astype(jnp.float32)
            col[2 * f + part, x, core] = (v * factor).astype(jnp.bfloat16)
            to_sib(2 * f + part).start()
            to_x(2 * f + part).start()

    n_src = col.shape[1] * col.shape[2]
    depth = n_src * 2 * windows
    scale = jnp.float32(1.0) / jnp.sqrt(jnp.float32(n_src * windows))

    def multiply(f, half):
        acc = lax.dot_general(
            srcs[half, pl.ds(2 * f, 2)].reshape(depth, channels),
            rhs[...].reshape(depth, 2 * channels),
            (((0,), (0,)), ((), ())),
            preferred_element_type=jnp.float32,
        )
        acc = (acc * scale).astype(jnp.bfloat16)
        stage[f, half, 0] = acc[:, :channels]
        stage[f, half, 1] = acc[:, channels:]
        put(f, half).start()

    def both(first, second):
        return jnp.logical_and(first, second)

    def along_own(f):
        @pl.when(is_root)
        def _():
            arrived(col.at[f, x, ocore], r_sib.at[f])
            srcs[y, f, x] = col[f, x]

        @pl.when(jnp.logical_not(is_root))
        def _():
            arrived(srcs.at[y, f, x], r_z.at[f])

        @pl.when(up_ok)
        def _():
            to_up(f).start()

        @pl.when(dn_ok)
        def _():
            to_dn(f).start()

        @pl.when(jnp.logical_or(is_root, f >= N_Y_ONCE))
        def _():
            to_ya(f).start()

    def along_transit(f):
        @pl.when(is_troot)
        def _():
            arrived(col.at[f, x, ocore], r_sib.at[f])
            transit[f] = col[f, x]

        @pl.when(jnp.logical_not(is_troot))
        def _():
            arrived(transit.at[f], r_t.at[f])

        @pl.when(tup_ok)
        def _():
            to_tup(f).start()

        @pl.when(tdn_ok)
        def _():
            to_tdn(f).start()

        @pl.when(jnp.logical_not(is_troot))
        def _():
            to_tx(f).start()

    def column(f):
        arrived(col.at[f, ox, core], r_x.at[f])
        fwd(f).start()

    def across_other(f):
        @pl.when(is_root)
        def _():
            arrived(col.at[f, ox, ocore], r_fwd.at[f])
            srcs[y, f, ox] = col[f, ox]

        @pl.when(jnp.logical_not(is_root))
        def _():
            arrived(srcs.at[y, f, ox], r_tx.at[f])

        to_yb(f).start()

    def across_once(f):
        arrived(srcs.at[oy, f, x], r_ya.at[f])

        @pl.when(up_ok)
        def _():
            to_up2(f).start()

        @pl.when(dn_ok)
        def _():
            to_dn2(f).start()

    def finish(f):
        @pl.when(jnp.logical_not(jnp.logical_or(is_root, is_troot)))
        def _():
            arrived(col.at[f, x, ocore], r_sib.at[f])

        @pl.when(jnp.logical_not(is_root))
        def _():
            arrived(col.at[f, ox, ocore], r_fwd.at[f])

        @pl.when(f >= N_Y_ONCE)
        def _():
            arrived(srcs.at[oy, f, x], r_ya.at[f])

        arrived(srcs.at[oy, f, ox], r_yb.at[f])

        @pl.when(lax.rem(f, 2) == 1)
        def _():
            real, imag = col[f - 1], col[f]
            rhs[0, :, :, :, :channels] = real
            rhs[1, :, :, :, :channels] = imag
            rhs[0, :, :, :, channels:] = imag
            rhs[1, :, :, :, channels:] = -real
            multiply(f // 2, 0)
            multiply(f // 2, 1)

    dist = HOP * jnp.where(z > s, z - s, s - z)
    tdist = HOP * jnp.where(z > xp, z - xp, xp - z)
    b_lag = HOP + jnp.where(is_root, HOP, dist)
    last = b_lag + HOP
    n_steps = chunks + HOP * (n_z + 1)

    def step(t, carry):
        for work, lag, count in (
            (along_own, dist, chunks),
            (along_transit, tdist, chunks),
            (column, 1, chunks),
            (across_once, dist + HOP, N_Y_ONCE),
            (across_other, b_lag, chunks),
            (finish, last, chunks),
        ):

            @pl.when(both(t >= lag, t < lag + count))
            def _(work=work, lag=lag):
                work(t - lag)

        return carry

    lax.fori_loop(0, n_steps, step, 0)

    def drain(f, carry):
        to_sib(f).wait_send()
        to_x(f).wait_send()
        fwd(f).wait_send()
        to_yb(f).wait_send()

        for sent, condition in (
            (to_up, up_ok),
            (to_dn, dn_ok),
            (to_ya, jnp.logical_or(is_root, f >= N_Y_ONCE)),
            (to_tup, tup_ok),
            (to_tdn, tdn_ok),
            (to_tx, jnp.logical_not(is_troot)),
            (to_up2, both(up_ok, f < N_Y_ONCE)),
            (to_dn2, both(dn_ok, f < N_Y_ONCE)),
        ):

            @pl.when(condition)
            def _(sent=sent):
                sent(f).wait_send()

        return carry

    lax.fori_loop(0, chunks, drain, 0)

    def stored(f, carry):
        put(f, 0).wait()
        put(f, 1).wait()
        return carry

    lax.fori_loop(0, bins, stored, 0)


def grid_body(n_z, spectra, alive):
    parts, bins, windows, channels = spectra.shape
    n_src = lax.axis_size("src")
    dma = pltpu.SemaphoreType.DMA
    rows = 2 * channels
    block = (2, windows, channels)
    chunks = parts * bins
    return pl.pallas_call(
        functools.partial(kernel, n_z),
        out_shape=jax.ShapeDtypeStruct((parts, bins, rows, channels), jnp.bfloat16),
        in_specs=[pl.BlockSpec(memory_space=pl.ANY)] * 2,
        out_specs=pl.BlockSpec(memory_space=pl.ANY),
        scratch_shapes=[
            pltpu.VMEM(spectra.shape, jnp.bfloat16),
            pltpu.VMEM(alive.shape, jnp.int32),
            pltpu.VMEM((chunks, 2) + block, jnp.bfloat16),
            pltpu.VMEM((2, chunks, 2) + block, jnp.bfloat16),
            pltpu.VMEM((chunks,) + block, jnp.bfloat16),
            pltpu.VMEM((parts, 2, 2, windows, 2 * channels), jnp.bfloat16),
            pltpu.VMEM((bins, 2, parts, channels, channels), jnp.bfloat16),
        ]
        + [dma((chunks,))] * 20
        + [dma((2,)), dma((bins, 2))],
        compiler_params=pltpu.CompilerParams(
            collective_id=0, has_side_effects=True, vmem_limit_bytes=60 * 2**20
        ),
        cost_estimate=pl.CostEstimate(
            flops=8 * bins * n_src * windows * rows * channels,
            bytes_accessed=10 * spectra.size * parts * n_src,
            transcendentals=0,
        ),
    )(spectra, alive)


def solution(mesh):
    if mesh.shape["src"] == 4 and mesh.shape["rcv"] == 8:
        body = functools.partial(grid_body, mesh.shape["rcv"] // 2)
    else:
        body = general_body
    return jax.shard_map(
        body,
        mesh=mesh,
        in_specs=(P(None, None, "src", "rcv"), P("src", "rcv")),
        out_specs=P(None, None, "src", "rcv"),
        check_vma=False,
    )
```

```python
import functools

import jax
import jax.numpy as jnp
from jax import lax
from jax.experimental import pallas as pl
from jax.experimental.pallas import tpu as pltpu
from jax.sharding import PartitionSpec as P

MESH = pl.DeviceIdType.MESH

N_Y_ONCE = 4
HOP = 2


def spread(block, axis, holder):
    block = jnp.where(lax.axis_index(axis) == holder, block, jnp.zeros_like(block))
    return lax.psum(block, axis)


def whiten(spectra, alive, bins):
    values = spectra.astype(jnp.float32)
    power = jnp.sum(values * values, axis=(0, 1)) / bins
    factor = alive.astype(jnp.float32) / jnp.sqrt(jnp.maximum(power, 0.5))
    return (values * factor).astype(jnp.bfloat16)


def cross_terms(source_part, receiver_part):
    swapped = jnp.stack((receiver_part[1], -receiver_part[0]))
    real_sum = jnp.einsum(
        "kfwc,kfwd->fcd", source_part, receiver_part, preferred_element_type=jnp.float32
    )
    imag_sum = jnp.einsum(
        "kfwc,kfwd->fcd", source_part, swapped, preferred_element_type=jnp.float32
    )
    return jnp.stack((real_sum, imag_sum))


def general_body(spectra, alive):
    bins = spectra.shape[1]
    whitened = whiten(spectra, alive, bins)
    ratio = lax.axis_size("rcv") // lax.axis_size("src")
    row_index = lax.axis_index("src")
    receivers = lax.all_gather(whitened, "src", axis=2, tiled=True)
    blocks = []
    for offset in range(ratio):
        blocks.append(spread(receivers, "rcv", row_index * ratio + offset))
    sources = jnp.concatenate(blocks, axis=3)
    stacked = cross_terms(sources, receivers)
    total_windows = receivers.shape[2]
    factor = jnp.float32(1.0) / jnp.sqrt(jnp.float32(total_windows))
    return (stacked * factor).astype(jnp.bfloat16)


def kernel(
    n_z,
    spectra_hbm,
    alive_hbm,
    out_ref,
    spectra_ref,
    alive_ref,
    col,
    srcs,
    transit,
    rhs,
    stage,
    r_sib,
    r_x,
    r_fwd,
    r_z,
    r_t,
    r_tx,
    r_ya,
    r_yb,
    s_sib,
    s_x,
    s_fwd,
    s_up,
    s_dn,
    s_tup,
    s_tdn,
    s_tx,
    s_ya,
    s_yb,
    s_up2,
    s_dn2,
    i_sem,
    o_sem,
):
    bins, windows, channels = spectra_ref.shape[1:]
    chunks = 2 * bins
    s = lax.axis_index("src")
    r = lax.axis_index("rcv")
    x = s // 2
    core = lax.rem(s, 2)
    y = lax.rem(r, 2)
    z = r // 2
    ox, ocore, oy = 1 - x, 1 - core, 1 - y
    sib = 2 * x + ocore
    xp = 2 * ox + core
    ry = r + 1 - 2 * y
    is_root = z == s
    is_troot = z == xp
    up_ok = jnp.logical_and(z >= s, z < n_z - 1)
    dn_ok = jnp.logical_and(z <= s, z > 0)
    tup_ok = jnp.logical_and(z >= xp, z < n_z - 1)
    tdn_ok = jnp.logical_and(z <= xp, z > 0)

    load_spectra = pltpu.make_async_copy(spectra_hbm, spectra_ref, i_sem.at[0])
    load_alive = pltpu.make_async_copy(alive_hbm, alive_ref, i_sem.at[1])
    load_spectra.start()
    load_alive.start()

    barrier = pltpu.get_barrier_semaphore()
    for target in ((sib, r), (xp, r), (s, ry)):
        pl.semaphore_signal(barrier, inc=1, device_id=target, device_id_type=MESH)

    @pl.when(z < n_z - 1)
    def _():
        pl.semaphore_signal(barrier, inc=1, device_id=(s, r + 2), device_id_type=MESH)

    @pl.when(z > 0)
    def _():
        pl.semaphore_signal(barrier, inc=1, device_id=(s, r - 2), device_id_type=MESH)

    load_spectra.wait()
    load_alive.wait()
    power = jnp.zeros((windows, channels), jnp.float32)
    for part in range(2):
        for f in range(bins):
            v = spectra_ref[part, f].astype(jnp.float32)
            power = power + v * v
    power = power / bins
    factor = alive_ref[...].astype(jnp.float32) / jnp.sqrt(jnp.maximum(power, 0.5))

    peers = 3 + jnp.where(z < n_z - 1, 1, 0) + jnp.where(z > 0, 1, 0)
    pl.semaphore_wait(barrier, peers)

    def remote(src, dst, send, recv, target):
        return pltpu.make_async_remote_copy(
            src_ref=src,
            dst_ref=dst,
            send_sem=send,
            recv_sem=recv,
            device_id=target,
            device_id_type=MESH,
        )

    above, below, across = (s, r + 2), (s, r - 2), (s, ry)

    def to_sib(f):
        block = col.at[f, x, core]
        return remote(block, block, s_sib.at[f], r_sib.at[f], (sib, r))

    def to_x(f):
        block = col.at[f, x, core]
        return remote(block, block, s_x.at[f], r_x.at[f], (xp, r))

    def fwd(f):
        block = col.at[f, ox, core]
        return remote(block, block, s_fwd.at[f], r_fwd.at[f], (sib, r))

    def to_up(f):
        block = srcs.at[y, f, x]
        return remote(block, block, s_up.at[f], r_z.at[f], above)

    def to_dn(f):
        block = srcs.at[y, f, x]
        return remote(block, block, s_dn.at[f], r_z.at[f], below)

    def to_ya(f):
        block = srcs.at[y, f, x]
        return remote(block, block, s_ya.at[f], r_ya.at[f], across)

    def to_yb(f):
        block = srcs.at[y, f, ox]
        return remote(block, block, s_yb.at[f], r_yb.at[f], across)

    def to_up2(f):
        block = srcs.at[oy, f, x]
        return remote(block, block, s_up2.at[f], r_ya.at[f], above)

    def to_dn2(f):
        block = srcs.at[oy, f, x]
        return remote(block, block, s_dn2.at[f], r_ya.at[f], below)

    def to_tup(f):
        return remote(transit.at[f], transit.at[f], s_tup.at[f], r_t.at[f], above)

    def to_tdn(f):
        return remote(transit.at[f], transit.at[f], s_tdn.at[f], r_t.at[f], below)

    def to_tx(f):
        block = srcs.at[y, f, x]
        return remote(transit.at[f], block, s_tx.at[f], r_tx.at[f], (xp, r))

    def arrived(ref, sem):
        remote(ref, ref, sem, sem, (sib, r)).wait_recv()

    def put(f, half):
        rows = pl.ds(pl.multiple_of(half * channels, channels), channels)
        return pltpu.make_async_copy(
            stage.at[f, half], out_ref.at[:, f, rows, :], o_sem.at[f, half]
        )

    for f in range(bins):
        for part in range(2):
            v = spectra_ref[part, f].astype(jnp.float32)
            col[2 * f + part, x, core] = (v * factor).astype(jnp.bfloat16)
            to_sib(2 * f + part).start()
            to_x(2 * f + part).start()

    n_src = col.shape[1] * col.shape[2]
    depth = n_src * 2 * windows
    scale = jnp.float32(1.0) / jnp.sqrt(jnp.float32(n_src * windows))

    def multiply(f, half):
        acc = lax.dot_general(
            srcs[half, pl.ds(2 * f, 2)].reshape(depth, channels),
            rhs[...].reshape(depth, 2 * channels),
            (((0,), (0,)), ((), ())),
            preferred_element_type=jnp.float32,
        )
        acc = (acc * scale).astype(jnp.bfloat16)
        stage[f, half, 0] = acc[:, :channels]
        stage[f, half, 1] = acc[:, channels:]
        put(f, half).start()

    def both(first, second):
        return jnp.logical_and(first, second)

    def along_own(f):
        @pl.when(is_root)
        def _():
            arrived(col.at[f, x, ocore], r_sib.at[f])
            srcs[y, f, x] = col[f, x]

        @pl.when(jnp.logical_not(is_root))
        def _():
            arrived(srcs.at[y, f, x], r_z.at[f])

        @pl.when(up_ok)
        def _():
            to_up(f).start()

        @pl.when(dn_ok)
        def _():
            to_dn(f).start()

        @pl.when(jnp.logical_or(is_root, f >= N_Y_ONCE))
        def _():
            to_ya(f).start()

    def along_transit(f):
        @pl.when(is_troot)
        def _():
            arrived(col.at[f, x, ocore], r_sib.at[f])
            transit[f] = col[f, x]

        @pl.when(jnp.logical_not(is_troot))
        def _():
            arrived(transit.at[f], r_t.at[f])

        @pl.when(tup_ok)
        def _():
            to_tup(f).start()

        @pl.when(tdn_ok)
        def _():
            to_tdn(f).start()

        @pl.when(jnp.logical_not(is_troot))
        def _():
            to_tx(f).start()

    def column(f):
        arrived(col.at[f, ox, core], r_x.at[f])
        fwd(f).start()

    def across_other(f):
        @pl.when(is_root)
        def _():
            arrived(col.at[f, ox, ocore], r_fwd.at[f])
            srcs[y, f, ox] = col[f, ox]

        @pl.when(jnp.logical_not(is_root))
        def _():
            arrived(srcs.at[y, f, ox], r_tx.at[f])

        to_yb(f).start()

    def across_once(f):
        arrived(srcs.at[oy, f, x], r_ya.at[f])

        @pl.when(up_ok)
        def _():
            to_up2(f).start()

        @pl.when(dn_ok)
        def _():
            to_dn2(f).start()

    def finish(f):
        @pl.when(jnp.logical_not(jnp.logical_or(is_root, is_troot)))
        def _():
            arrived(col.at[f, x, ocore], r_sib.at[f])

        @pl.when(jnp.logical_not(is_root))
        def _():
            arrived(col.at[f, ox, ocore], r_fwd.at[f])

        @pl.when(f >= N_Y_ONCE)
        def _():
            arrived(srcs.at[oy, f, x], r_ya.at[f])

        arrived(srcs.at[oy, f, ox], r_yb.at[f])

        @pl.when(lax.rem(f, 2) == 1)
        def _():
            real, imag = col[f - 1], col[f]
            rhs[0, :, :, :, :channels] = real
            rhs[1, :, :, :, :channels] = imag
            rhs[0, :, :, :, channels:] = imag
            rhs[1, :, :, :, channels:] = -real
            multiply(f // 2, 0)
            multiply(f // 2, 1)

    @pl.when(is_root)
    def _():
        lax.fori_loop(0, chunks, lambda f, carry: (along_own(f), carry)[1], 0)

    @pl.when(is_troot)
    def _():
        lax.fori_loop(0, chunks, lambda f, carry: (along_transit(f), carry)[1], 0)

    dist = HOP * jnp.where(z > s, z - s, s - z)
    tdist = HOP * jnp.where(z > xp, z - xp, xp - z)
    b_lag = jnp.where(is_root, HOP, dist)
    n_steps = chunks + HOP * n_z

    def step(t, carry):
        for work, lag, count, active in (
            (along_own, dist - HOP, chunks, jnp.logical_not(is_root)),
            (along_transit, tdist - HOP, chunks, jnp.logical_not(is_troot)),
            (column, 0, chunks, True),
            (across_once, dist, N_Y_ONCE, True),
            (across_other, b_lag, chunks, True),
            (finish, b_lag + HOP, chunks, True),
        ):

            @pl.when(both(active, both(t >= lag, t < lag + count)))
            def _(work=work, lag=lag):
                work(t - lag)

        return carry

    lax.fori_loop(0, n_steps, step, 0)

    def drain(f, carry):
        to_sib(f).wait_send()
        to_x(f).wait_send()
        fwd(f).wait_send()
        to_yb(f).wait_send()

        for sent, condition in (
            (to_up, up_ok),
            (to_dn, dn_ok),
            (to_ya, jnp.logical_or(is_root, f >= N_Y_ONCE)),
            (to_tup, tup_ok),
            (to_tdn, tdn_ok),
            (to_tx, jnp.logical_not(is_troot)),
            (to_up2, both(up_ok, f < N_Y_ONCE)),
            (to_dn2, both(dn_ok, f < N_Y_ONCE)),
        ):

            @pl.when(condition)
            def _(sent=sent):
                sent(f).wait_send()

        return carry

    lax.fori_loop(0, chunks, drain, 0)

    def stored(f, carry):
        put(f, 0).wait()
        put(f, 1).wait()
        return carry

    lax.fori_loop(0, bins, stored, 0)


def grid_body(n_z, spectra, alive):
    parts, bins, windows, channels = spectra.shape
    n_src = lax.axis_size("src")
    dma = pltpu.SemaphoreType.DMA
    rows = 2 * channels
    block = (2, windows, channels)
    chunks = parts * bins
    return pl.pallas_call(
        functools.partial(kernel, n_z),
        out_shape=jax.ShapeDtypeStruct((parts, bins, rows, channels), jnp.bfloat16),
        in_specs=[pl.BlockSpec(memory_space=pltpu.HBM)] * 2,
        out_specs=pl.BlockSpec(memory_space=pl.ANY),
        scratch_shapes=[
            pltpu.VMEM(spectra.shape, jnp.bfloat16),
            pltpu.VMEM(alive.shape, jnp.int32),
            pltpu.VMEM((chunks, 2) + block, jnp.bfloat16),
            pltpu.VMEM((2, chunks, 2) + block, jnp.bfloat16),
            pltpu.VMEM((chunks,) + block, jnp.bfloat16),
            pltpu.VMEM((parts, 2, 2, windows, 2 * channels), jnp.bfloat16),
            pltpu.VMEM((bins, 2, parts, channels, channels), jnp.bfloat16),
        ]
        + [dma((chunks,))] * 20
        + [dma((2,)), dma((bins, 2))],
        compiler_params=pltpu.CompilerParams(
            collective_id=0, has_side_effects=True, vmem_limit_bytes=48 * 2**20
        ),
        cost_estimate=pl.CostEstimate(
            flops=8 * bins * n_src * windows * rows * channels,
            bytes_accessed=10 * spectra.size * parts * n_src,
            transcendentals=0,
        ),
    )(spectra, alive)


def solution(mesh):
    if mesh.shape["src"] == 4 and mesh.shape["rcv"] == 8:
        body = functools.partial(grid_body, mesh.shape["rcv"] // 2)
    else:
        body = general_body
    return jax.shard_map(
        body,
        mesh=mesh,
        in_specs=(P(None, None, "src", "rcv"), P("src", "rcv")),
        out_specs=P(None, None, "src", "rcv"),
        check_vma=False,
    )
```

```python
import functools

import jax
import jax.numpy as jnp
from jax import lax
from jax.experimental import pallas as pl
from jax.experimental.pallas import tpu as pltpu
from jax.sharding import PartitionSpec as P

MESH = pl.DeviceIdType.MESH

N_Y_ONCE = 4
HOP = 2


def spread(block, axis, holder):
    block = jnp.where(lax.axis_index(axis) == holder, block, jnp.zeros_like(block))
    return lax.psum(block, axis)


def whiten(spectra, alive, bins):
    values = spectra.astype(jnp.float32)
    power = jnp.sum(values * values, axis=(0, 1)) / bins
    factor = alive.astype(jnp.float32) / jnp.sqrt(jnp.maximum(power, 0.5))
    return (values * factor).astype(jnp.bfloat16)


def cross_terms(source_part, receiver_part):
    swapped = jnp.stack((receiver_part[1], -receiver_part[0]))
    real_sum = jnp.einsum(
        "kfwc,kfwd->fcd", source_part, receiver_part, preferred_element_type=jnp.float32
    )
    imag_sum = jnp.einsum(
        "kfwc,kfwd->fcd", source_part, swapped, preferred_element_type=jnp.float32
    )
    return jnp.stack((real_sum, imag_sum))


def general_body(spectra, alive):
    bins = spectra.shape[1]
    whitened = whiten(spectra, alive, bins)
    ratio = lax.axis_size("rcv") // lax.axis_size("src")
    row_index = lax.axis_index("src")
    receivers = lax.all_gather(whitened, "src", axis=2, tiled=True)
    blocks = []
    for offset in range(ratio):
        blocks.append(spread(receivers, "rcv", row_index * ratio + offset))
    sources = jnp.concatenate(blocks, axis=3)
    stacked = cross_terms(sources, receivers)
    total_windows = receivers.shape[2]
    factor = jnp.float32(1.0) / jnp.sqrt(jnp.float32(total_windows))
    return (stacked * factor).astype(jnp.bfloat16)


def kernel(
    n_z,
    spectra_ref,
    alive_ref,
    out_ref,
    col,
    srcs,
    transit,
    rhs,
    stage,
    r_sib,
    r_x,
    r_fwd,
    r_z,
    r_t,
    r_tx,
    r_ya,
    r_yb,
    s_sib,
    s_x,
    s_fwd,
    s_up,
    s_dn,
    s_tup,
    s_tdn,
    s_tx,
    s_ya,
    s_yb,
    s_up2,
    s_dn2,
    o_sem,
):
    bins, windows, channels = spectra_ref.shape[1:]
    chunks = 2 * bins
    s = lax.axis_index("src")
    r = lax.axis_index("rcv")
    x = s // 2
    core = lax.rem(s, 2)
    y = lax.rem(r, 2)
    z = r // 2
    ox, ocore, oy = 1 - x, 1 - core, 1 - y
    sib = 2 * x + ocore
    xp = 2 * ox + core
    ry = r + 1 - 2 * y
    is_root = z == s
    is_troot = z == xp
    up_ok = jnp.logical_and(z >= s, z < n_z - 1)
    dn_ok = jnp.logical_and(z <= s, z > 0)
    tup_ok = jnp.logical_and(z >= xp, z < n_z - 1)
    tdn_ok = jnp.logical_and(z <= xp, z > 0)

    barrier = pltpu.get_barrier_semaphore()
    for target in ((sib, r), (xp, r), (s, ry)):
        pl.semaphore_signal(barrier, inc=1, device_id=target, device_id_type=MESH)

    @pl.when(z < n_z - 1)
    def _():
        pl.semaphore_signal(barrier, inc=1, device_id=(s, r + 2), device_id_type=MESH)

    @pl.when(z > 0)
    def _():
        pl.semaphore_signal(barrier, inc=1, device_id=(s, r - 2), device_id_type=MESH)

    power = jnp.zeros((windows, channels), jnp.float32)
    for part in range(2):
        for f in range(bins):
            v = spectra_ref[part, f].astype(jnp.float32)
            power = power + v * v
    power = power / bins
    factor = alive_ref[...].astype(jnp.float32) / jnp.sqrt(jnp.maximum(power, 0.5))

    peers = 3 + jnp.where(z < n_z - 1, 1, 0) + jnp.where(z > 0, 1, 0)
    pl.semaphore_wait(barrier, peers)

    def remote(src, dst, send, recv, target):
        return pltpu.make_async_remote_copy(
            src_ref=src,
            dst_ref=dst,
            send_sem=send,
            recv_sem=recv,
            device_id=target,
            device_id_type=MESH,
        )

    above, below, across = (s, r + 2), (s, r - 2), (s, ry)

    def to_sib(f):
        block = col.at[f, x, core]
        return remote(block, block, s_sib.at[f], r_sib.at[f], (sib, r))

    def to_x(f):
        block = col.at[f, x, core]
        return remote(block, block, s_x.at[f], r_x.at[f], (xp, r))

    def fwd(f):
        block = col.at[f, ox, core]
        return remote(block, block, s_fwd.at[f], r_fwd.at[f], (sib, r))

    def to_up(f):
        block = srcs.at[y, f, x]
        return remote(block, block, s_up.at[f], r_z.at[f], above)

    def to_dn(f):
        block = srcs.at[y, f, x]
        return remote(block, block, s_dn.at[f], r_z.at[f], below)

    def to_ya(f):
        block = srcs.at[y, f, x]
        return remote(block, block, s_ya.at[f], r_ya.at[f], across)

    def to_yb(f):
        block = srcs.at[y, f, ox]
        return remote(block, block, s_yb.at[f], r_yb.at[f], across)

    def to_up2(f):
        block = srcs.at[oy, f, x]
        return remote(block, block, s_up2.at[f], r_ya.at[f], above)

    def to_dn2(f):
        block = srcs.at[oy, f, x]
        return remote(block, block, s_dn2.at[f], r_ya.at[f], below)

    def to_tup(f):
        return remote(transit.at[f], transit.at[f], s_tup.at[f], r_t.at[f], above)

    def to_tdn(f):
        return remote(transit.at[f], transit.at[f], s_tdn.at[f], r_t.at[f], below)

    def to_tx(f):
        block = srcs.at[y, f, x]
        return remote(transit.at[f], block, s_tx.at[f], r_tx.at[f], (xp, r))

    def arrived(ref, sem):
        remote(ref, ref, sem, sem, (sib, r)).wait_recv()

    def put(f, half):
        rows = pl.ds(pl.multiple_of(half * channels, channels), channels)
        return pltpu.make_async_copy(
            stage.at[f, half], out_ref.at[:, f, rows, :], o_sem.at[f, half]
        )

    for f in range(bins):
        for part in range(2):
            v = spectra_ref[part, f].astype(jnp.float32)
            col[2 * f + part, x, core] = (v * factor).astype(jnp.bfloat16)
            to_sib(2 * f + part).start()
            to_x(2 * f + part).start()

    n_src = col.shape[1] * col.shape[2]
    depth = n_src * 2 * windows
    scale = jnp.float32(1.0) / jnp.sqrt(jnp.float32(n_src * windows))

    def multiply(f, half):
        acc = lax.dot_general(
            srcs[half, pl.ds(2 * f, 2)].reshape(depth, channels),
            rhs[...].reshape(depth, 2 * channels),
            (((0,), (0,)), ((), ())),
            preferred_element_type=jnp.float32,
        )
        acc = (acc * scale).astype(jnp.bfloat16)
        stage[f, half, 0] = acc[:, :channels]
        stage[f, half, 1] = acc[:, channels:]
        put(f, half).start()

    def both(first, second):
        return jnp.logical_and(first, second)

    def along_own(f):
        @pl.when(is_root)
        def _():
            arrived(col.at[f, x, ocore], r_sib.at[f])
            srcs[y, f, x] = col[f, x]

        @pl.when(jnp.logical_not(is_root))
        def _():
            arrived(srcs.at[y, f, x], r_z.at[f])

        @pl.when(up_ok)
        def _():
            to_up(f).start()

        @pl.when(dn_ok)
        def _():
            to_dn(f).start()

        @pl.when(jnp.logical_or(is_root, f >= N_Y_ONCE))
        def _():
            to_ya(f).start()

    def along_transit(f):
        @pl.when(is_troot)
        def _():
            arrived(col.at[f, x, ocore], r_sib.at[f])
            transit[f] = col[f, x]

        @pl.when(jnp.logical_not(is_troot))
        def _():
            arrived(transit.at[f], r_t.at[f])

        @pl.when(tup_ok)
        def _():
            to_tup(f).start()

        @pl.when(tdn_ok)
        def _():
            to_tdn(f).start()

        @pl.when(jnp.logical_not(is_troot))
        def _():
            to_tx(f).start()

    def column(f):
        arrived(col.at[f, ox, core], r_x.at[f])
        fwd(f).start()

    def across_other(f):
        @pl.when(is_root)
        def _():
            arrived(col.at[f, ox, ocore], r_fwd.at[f])
            srcs[y, f, ox] = col[f, ox]

        @pl.when(jnp.logical_not(is_root))
        def _():
            arrived(srcs.at[y, f, ox], r_tx.at[f])

        to_yb(f).start()

    def across_once(f):
        arrived(srcs.at[oy, f, x], r_ya.at[f])

        @pl.when(up_ok)
        def _():
            to_up2(f).start()

        @pl.when(dn_ok)
        def _():
            to_dn2(f).start()

    def finish(f):
        @pl.when(jnp.logical_not(jnp.logical_or(is_root, is_troot)))
        def _():
            arrived(col.at[f, x, ocore], r_sib.at[f])

        @pl.when(jnp.logical_not(is_root))
        def _():
            arrived(col.at[f, ox, ocore], r_fwd.at[f])

        @pl.when(f >= N_Y_ONCE)
        def _():
            arrived(srcs.at[oy, f, x], r_ya.at[f])

        arrived(srcs.at[oy, f, ox], r_yb.at[f])

        @pl.when(lax.rem(f, 2) == 1)
        def _():
            real, imag = col[f - 1], col[f]
            rhs[0, :, :, :, :channels] = real
            rhs[1, :, :, :, :channels] = imag
            rhs[0, :, :, :, channels:] = imag
            rhs[1, :, :, :, channels:] = -real
            multiply(f // 2, 0)
            multiply(f // 2, 1)

    dist = HOP * jnp.where(z > s, z - s, s - z)
    tdist = HOP * jnp.where(z > xp, z - xp, xp - z)
    b_lag = HOP + jnp.where(is_root, HOP, dist)
    last = b_lag + HOP
    n_steps = chunks + HOP * (n_z + 1)

    def step(t, carry):
        for work, lag, count in (
            (along_own, dist, chunks),
            (along_transit, tdist, chunks),
            (column, 1, chunks),
            (across_once, dist + HOP, N_Y_ONCE),
            (across_other, b_lag, chunks),
            (finish, last, chunks),
        ):

            @pl.when(both(t >= lag, t < lag + count))
            def _(work=work, lag=lag):
                work(t - lag)

        return carry

    lax.fori_loop(0, n_steps, step, 0)

    def drain(f, carry):
        to_sib(f).wait_send()
        to_x(f).wait_send()
        fwd(f).wait_send()
        to_yb(f).wait_send()

        for sent, condition in (
            (to_up, up_ok),
            (to_dn, dn_ok),
            (to_ya, jnp.logical_or(is_root, f >= N_Y_ONCE)),
            (to_tup, tup_ok),
            (to_tdn, tdn_ok),
            (to_tx, jnp.logical_not(is_troot)),
            (to_up2, both(up_ok, f < N_Y_ONCE)),
            (to_dn2, both(dn_ok, f < N_Y_ONCE)),
        ):

            @pl.when(condition)
            def _(sent=sent):
                sent(f).wait_send()

        return carry

    lax.fori_loop(0, chunks, drain, 0)

    def stored(f, carry):
        put(f, 0).wait()
        put(f, 1).wait()
        return carry

    lax.fori_loop(0, bins, stored, 0)


def grid_body(n_z, spectra, alive):
    parts, bins, windows, channels = spectra.shape
    n_src = lax.axis_size("src")
    dma = pltpu.SemaphoreType.DMA
    rows = 2 * channels
    block = (2, windows, channels)
    chunks = parts * bins
    return pl.pallas_call(
        functools.partial(kernel, n_z),
        out_shape=jax.ShapeDtypeStruct((parts, bins, rows, channels), jnp.bfloat16),
        in_specs=[pl.BlockSpec(memory_space=pltpu.VMEM)] * 2,
        out_specs=pl.BlockSpec(memory_space=pl.ANY),
        scratch_shapes=[
            pltpu.VMEM((chunks, 2) + block, jnp.bfloat16),
            pltpu.VMEM((2, chunks, 2) + block, jnp.bfloat16),
            pltpu.VMEM((chunks,) + block, jnp.bfloat16),
            pltpu.VMEM((parts, 2, 2, windows, 2 * channels), jnp.bfloat16),
            pltpu.VMEM((bins, 2, parts, channels, channels), jnp.bfloat16),
        ]
        + [dma((chunks,))] * 20
        + [dma((bins, 2))],
        compiler_params=pltpu.CompilerParams(
            collective_id=0, has_side_effects=True, vmem_limit_bytes=48 * 2**20
        ),
        cost_estimate=pl.CostEstimate(
            flops=8 * bins * n_src * windows * rows * channels,
            bytes_accessed=10 * spectra.size * parts * n_src,
            transcendentals=0,
        ),
    )(spectra, alive)


def solution(mesh):
    if mesh.shape["src"] == 4 and mesh.shape["rcv"] == 8:
        body = functools.partial(grid_body, mesh.shape["rcv"] // 2)
    else:
        body = general_body
    return jax.shard_map(
        body,
        mesh=mesh,
        in_specs=(P(None, None, "src", "rcv"), P("src", "rcv")),
        out_specs=P(None, None, "src", "rcv"),
        check_vma=False,
    )
```
